256 devices in a mesh: src: 16 (over y, x), tgt: 16 (over z, core).
Axes of the slice: x: 4, y: 4, z: 8, core: 2. Of those that a mesh axis runs over, the one named last changes fastest.
Arguments:
- log_kernel: bfloat16 [16, 16, 48, 256, 256], P('src', 'tgt'), may hold values from -8 to 320
- tile_rows: int32 [16, 16, 48], P('src', 'tgt'), may hold values from 0 to 127, as said below
- tile_cols: int32 [16, 16, 48], P('src', 'tgt'), may hold values from 0 to 127
- tile_count: int32 [16, 16], P('src', 'tgt'), may hold values from 1 to 48, as said below
- log_a: float32 [524288], P('src'), may hold values from -5 to 5
- log_b: float32 [524288], P('tgt'), may hold values from -5 to 5
- g_start: float32 [524288], P('tgt'), may hold values from -5 to 5
Outputs:
- source_pot: float32 [524288], P('src')
- target_pot: float32 [524288], P('tgt')
The draws below stay inside these ranges and needn't reach their ends.
Inputs may be any that keep to these rules, and one draw needn't show every extreme that they name: `tile_rows`: the first tile_count slots of a device name distinct row and column block pairs; the live tiles of all devices together contain every source row and every target column; slots past tile_count hold ids that are not used. `tile_count`: some device has all 48 slots live.
All inputs are finite; a program needn't handle non-finite values.
Results may differ from the reference program's by a relative error of at most 0.0003.
Values sent between devices are 32-bit elements; how exact they have to be, the bound alone decides.
A program may use at most 64 MiB of HBM per device.

```python
import jax
import jax.numpy as jnp
from jax import lax

BLK = 256
RB_DEV = 128
CB_DEV = 128
TILES = 48
ITERS = 2
NS = 524288
NT = 524288
N_SRC = 16
N_TGT = 16


def forced_layout():
    row_total = RB_DEV * N_SRC
    col_total = CB_DEV * N_TGT
    row_ids = jnp.arange(row_total, dtype=jnp.int32)
    col_for_row = (row_ids // RB_DEV + row_ids) % N_TGT * CB_DEV + row_ids // N_TGT % CB_DEV
    col_ids = jnp.arange(col_total, dtype=jnp.int32)
    row_for_col = (col_ids // CB_DEV + col_ids) % N_SRC * RB_DEV + col_ids // N_SRC % RB_DEV
    forced = jnp.zeros((row_total, col_total), jnp.int32)
    forced = forced.at[row_ids, col_for_row].set(1).at[row_for_col, col_ids].set(1)
    forced = forced.reshape(N_SRC, RB_DEV, N_TGT, CB_DEV).transpose(0, 2, 1, 3)
    return forced.reshape(N_SRC * N_TGT, RB_DEV * CB_DEV)


def tile_layout(key):
    forced = forced_layout()
    devices = N_SRC * N_TGT
    keys = jax.random.split(jax.random.fold_in(key, 11), devices)

    def arrange(sub_key, marks):
        ranks = jax.random.permutation(sub_key, RB_DEV * CB_DEV).astype(jnp.int32)
        scores = jnp.where(marks > 0, 0, 1 + ranks)
        return jnp.argsort(scores, stable=True)[:TILES].astype(jnp.int32)
    order = jax.vmap(arrange)(keys, forced)
    drawn = jax.random.randint(jax.random.fold_in(key, 12), (devices,), TILES // 4, TILES + 1).astype(jnp.int32)
    needed = jnp.sum(forced, axis=1).astype(jnp.int32)
    counts = jnp.maximum(drawn, needed).at[0].set(TILES)
    rows = (order // CB_DEV).reshape(N_SRC, N_TGT, TILES)
    cols = (order % CB_DEV).reshape(N_SRC, N_TGT, TILES)
    return (rows, cols, counts.reshape(N_SRC, N_TGT))


def draw_tile_rows(key, part):
    return tile_layout(key)[0]


def draw_tile_cols(key, part):
    return tile_layout(key)[1]


def draw_tile_count(key, part):
    return tile_layout(key)[2]


def draw_log_kernel(key, part):
    key = jax.random.fold_in(key, 5)
    shape = (N_SRC, N_TGT, TILES, BLK, BLK)
    values = 2.0 * jax.random.normal(key, shape, jnp.float32)
    return jnp.clip(values, -8.0, 8.0).astype(jnp.bfloat16)


def block_scale(own_key, shape, cuts, least, largest):
    factor_of = 1.0
    for position, parts in cuts:
        steps = jax.random.uniform(jax.random.fold_in(jax.random.fold_in(own_key, 6), position), (parts,), jnp.float32, least / len(cuts), largest / len(cuts))
        factor_of = factor_of * jnp.repeat(jnp.exp(steps), shape[position] // parts).reshape((-1,) + (1,) * (len(shape) - 1 - position))
    return factor_of


def gaussian(key, shape, scale, reach, shards=(), kind=jnp.bfloat16):
    loudness = block_scale(key, shape, shards, -0.22, 0.18) if shards else 1.0
    entries = jax.random.normal(key, shape, jnp.float32) * scale * loudness
    return jnp.minimum(jnp.maximum(entries, -reach), reach).astype(kind)


def setup_inputs(seed: int = 0) -> dict:
    splits = jax.random.split(jax.random.key(seed), 8)
    log_kernel = draw_log_kernel(jax.random.fold_in(splits[7], 71), 0)
    tile_rows = draw_tile_rows(jax.random.fold_in(splits[7], 71), 0)
    tile_cols = draw_tile_cols(jax.random.fold_in(splits[7], 71), 0)
    tile_count = draw_tile_count(jax.random.fold_in(splits[7], 71), 0)
    log_a = gaussian(splits[4], (NS,), 1.0, 5.0, ((0, 16),), jnp.float32)
    log_b = gaussian(splits[5], (NT,), 1.0, 5.0, ((0, 16),), jnp.float32)
    g_start = gaussian(splits[6], (NT,), 1.0, 5.0, ((0, 16),), jnp.float32)
    return {"log_kernel": log_kernel, "tile_rows": tile_rows, "tile_cols": tile_cols, "tile_count": tile_count, "log_a": log_a, "log_b": log_b, "g_start": g_start}


NEG = -1e30


def fold_blocks(tile_max, tile_sum, block_ids, is_live, nfold):
    onehot = (block_ids[:, None] == jnp.arange(nfold)[None, :]) & is_live[:, None]
    block_max = jnp.max(jnp.where(onehot[:, :, None], tile_max[:, None, :], NEG), axis=0)
    weight = onehot.astype(jnp.float32)
    spread = jnp.einsum("tr,rb->tb", weight, block_max, precision=lax.Precision.HIGHEST)
    scaled = tile_sum * jnp.exp(tile_max - spread)
    block_sum = jnp.einsum("tr,tb->rb", weight, scaled, precision=lax.Precision.HIGHEST)
    return block_max, block_sum


def tile_partials(kernel, fold_ids, pick_ids, is_live, vector, nfold, along_rows):
    selector = (pick_ids[:, None] == jnp.arange(vector.shape[0])[None, :]).astype(jnp.float32)
    selected = jnp.einsum("tc,cb->tb", selector, vector, precision=lax.Precision.HIGHEST)
    widened = kernel.astype(jnp.float32)
    if along_rows:
        shifted = widened + selected[:, None, :]
        reduce_axis = 2
    else:
        shifted = widened + selected[:, :, None]
        reduce_axis = 1
    tile_max = jnp.max(shifted, axis=reduce_axis)
    tile_sum = jnp.sum(jnp.exp(shifted - jnp.expand_dims(tile_max, reduce_axis)), axis=reduce_axis)
    tile_max = jnp.where(is_live[:, None], tile_max, NEG)
    tile_sum = jnp.where(is_live[:, None], tile_sum, 0.0)
    return fold_blocks(tile_max, tile_sum, fold_ids, is_live, nfold)


def settle(block_max, block_sum, reduce_axis):
    highest = jnp.max(block_max, axis=reduce_axis)
    summed = jnp.sum(block_sum * jnp.exp(block_max - jnp.expand_dims(highest, reduce_axis)), axis=reduce_axis)
    return highest + jnp.log(summed)


def reference(log_kernel, tile_rows, tile_cols, tile_count, log_a, log_b, g_start):
    devices = N_SRC * N_TGT
    kernels = log_kernel.reshape(devices, TILES, BLK, BLK)
    row_ids = tile_rows.reshape(devices, TILES)
    col_ids = tile_cols.reshape(devices, TILES)
    counts = tile_count.reshape(devices)
    device_ids = jnp.arange(devices, dtype=jnp.int32)
    source_log = log_a.reshape(N_SRC, RB_DEV, BLK)
    target_log = log_b.reshape(N_TGT, CB_DEV, BLK)
    target_pot = g_start.reshape(N_TGT, CB_DEV, BLK)
    source_pot = source_log
    for sweep_index in range(ITERS):
        def row_side(payload):
            kernel, row_part, col_part, live_count, device = payload
            is_live = jnp.arange(TILES) < live_count
            vector = target_pot[device % N_TGT]
            return tile_partials(kernel, row_part, col_part, is_live, vector, RB_DEV, True)

        block_max, block_sum = lax.map(row_side, (kernels, row_ids, col_ids, counts, device_ids))
        block_max = block_max.reshape(N_SRC, N_TGT, RB_DEV, BLK)
        block_sum = block_sum.reshape(N_SRC, N_TGT, RB_DEV, BLK)
        source_pot = source_log - settle(block_max, block_sum, 1)

        def col_side(payload):
            kernel, row_part, col_part, live_count, device = payload
            is_live = jnp.arange(TILES) < live_count
            vector = source_pot[device // N_TGT]
            return tile_partials(kernel, col_part, row_part, is_live, vector, CB_DEV, False)

        block_max, block_sum = lax.map(col_side, (kernels, row_ids, col_ids, counts, device_ids))
        block_max = block_max.reshape(N_SRC, N_TGT, CB_DEV, BLK)
        block_sum = block_sum.reshape(N_SRC, N_TGT, CB_DEV, BLK)
        target_pot = target_log - settle(block_max, block_sum, 0)
    return source_pot.reshape(NS), target_pot.reshape(NT)
```

```python
import functools

import jax
import jax.numpy as jnp
from jax import lax
from jax.experimental import pallas as pl
from jax.experimental.pallas import tpu as pltpu
from jax.sharding import PartitionSpec as P

ITERS = 2
TINY = 1e-37
LOG2E = 1.4426950408889634
LN2 = 0.6931471805599453
MESH = pl.DeviceIdType.MESH
GROUP = 4
CHUNK = 4

SPREAD = 8.0


def lse2(values):
    top = jnp.max(values, axis=0)
    total = jnp.sum(jnp.exp2(values - top[None]), axis=0)
    return top + log2(total)


def membership(ids_ref, count, into, back):
    slots = ids_ref.shape[1]
    block = lax.broadcasted_iota(jnp.int32, (128, slots), 0)
    slot = lax.broadcasted_iota(jnp.int32, (128, slots), 1)
    hit = (ids_ref[...] == block) & (slot < count)
    hit = jnp.where(hit, 1.0, 0.0)
    into[...] = hit.astype(jnp.bfloat16)
    back[...] = hit.T.astype(jnp.bfloat16)


def dot(a, b):
    return jnp.dot(a, b, preferred_element_type=jnp.float32)


def log2(x):
    return jnp.log(x) * LOG2E


def whole(
    n_src, n_tgt,
    k_hbm, rows_ref, cols_ref, count_ref, la_hbm, lb_hbm, g0_hbm,
    f_out, g_out,
    kb, kt, kf, pots, parts, rs_row, rs_col, la_v, lb_v, lb_other, g_own, g_last, g_raw, gathered, wide0, wide1, mrun, srun, f_nat,
    into_r, back_r, into_c, back_c, k_sem, in_sem, out_sem, lb_sem, lb_rsem, rs_send, rs_recv, ag_send, ag_recv,
):
    s, t = lax.axis_index("src"), lax.axis_index("tgt")
    z, c = t // 2, t % 2
    slots = kb.shape[0]
    n_chunks = slots // CHUNK
    n_z = n_tgt // 2
    r_rows = 128 // n_z
    c_rows = 128 // n_src

    def k_copy(i):
        piece = pl.ds(i * CHUNK, CHUNK)
        return pltpu.make_async_copy(k_hbm.at[piece], kb.at[piece], k_sem.at[i])

    g0_copy = pltpu.make_async_copy(g0_hbm, g_raw, in_sem.at[0])
    g0_copy.start()
    la_copy = pltpu.make_async_copy(la_hbm.at[pl.ds(2 * z * r_rows, 2 * r_rows)], la_v, in_sem.at[1])
    la_copy.start()
    lb_copy = pltpu.make_async_copy(lb_hbm.at[pl.ds(2 * s * c_rows, 2 * c_rows)], lb_v, in_sem.at[2])
    lb_copy.start()
    for i in range(n_chunks):
        k_copy(i).start()

    def row_hub(d):
        return (s, 2 * ((z + d) % n_z) + 1)

    def row_low(d):
        return (s, 2 * ((z + d) % n_z))

    def col_hub(d):
        return ((s + d) % n_src, 2 * z + 1)

    def col_low(d):
        return ((s + d) % n_src, 2 * z)

    barrier = pltpu.get_barrier_semaphore()

    def greet(peer):
        pl.semaphore_signal(barrier, inc=1, device_id=peer, device_id_type=MESH)

    @pl.when(c == 1)
    def _():
        for d in range(1, n_z):
            greet(row_hub(d))
            greet(row_low(d))
        for d in range(1, n_src):
            greet(col_hub(d))
            greet(col_low(d))
        greet((s, 2 * z))

    @pl.when(c == 0)
    def _():
        for d in range(1, n_z):
            greet(row_hub(d))
        for d in range(1, n_src):
            greet(col_hub(d))
        greet((s, 2 * z + 1))

    count = count_ref[0, 0]
    membership(rows_ref, count, into_r, back_r)
    membership(cols_ref, count, into_c, back_c)

    def blocks_of(ref, rows):
        return jnp.stack([ref[pl.ds(h, rows, stride=2), :] for h in (0, 1)])

    g0_copy.wait()
    pots[0] = blocks_of(g_raw, 128) * LOG2E
    la_copy.wait()
    lb_copy.wait()

    def prepare(i, carry):
        k_copy(i).wait()
        for u in range(CHUNK):
            slot = i * CHUNK + u
            for p in (0, 1):
                for q in (0, 1):
                    piece = kb[slot, 128 * p : 128 * p + 128, 128 * q : 128 * q + 128]
                    kf[slot, 128 * p : 128 * p + 128, 128 * q : 128 * q + 128] = piece.astype(jnp.float32) * LOG2E
                    flipped = piece.T.astype(jnp.float32) * LOG2E
                    kt[slot, 128 * q : 128 * q + 128, 128 * p : 128 * p + 128] = flipped
        return carry

    def sweep(tiles, pot, pick, into, back, part):
        def widen(wide, slot):
            for u in range(GROUP):
                for q in (0, 1):
                    row = gathered[pl.ds(q * slots + jnp.minimum(slot + u, slots - 1), 1), :]
                    wide[u, 128 * q : 128 * q + 128, :] = jnp.broadcast_to(row, (128, 128)).T

        def add_up(wide, slot, low):
            for u in range(GROUP):
                for h in (0, 1):
                    x = tiles[slot + u, :, 128 * h : 128 * h + 128] + wide[u]
                    x = x.reshape(32, 8, 128)
                    top = jnp.maximum(jnp.max(x, axis=0), mrun[low, :])
                    here = pl.ds(pl.multiple_of((slot + u) * 16 + 8 * h, 8), 8)
                    mrun[here, :] = top
                    srun[here, :] = jnp.sum(jnp.exp2(x - top[None]), axis=0)

        def step(i, carry):
            slot = i * (2 * GROUP)
            low = pl.ds(pl.multiple_of(16 * slots + 8 * jnp.maximum(i - slots, 0), 8), 8)
            widen(wide1, slot + GROUP)
            add_up(wide0, slot, low)
            widen(wide0, slot + 2 * GROUP)
            add_up(wide1, slot + GROUP, low)
            return carry

        mrun[16 * slots : 16 * slots + 8, :] = jnp.full((8, 128), -1e30, jnp.float32)
        value = jnp.concatenate([pot[0], pot[1]], axis=1)
        rows = jnp.zeros((slots, 256), jnp.float32)
        for _ in range(3):
            part_of = value.astype(jnp.bfloat16)
            rows += dot(pick[...], part_of)
            value -= part_of.astype(jnp.float32)
        for q in (0, 1):
            gathered[q * slots : (q + 1) * slots, :] = rows[:, 128 * q : 128 * q + 128]
        widen(wide0, 0)
        lax.fori_loop(0, slots // (2 * GROUP), step, 0)

        def over_sublanes(i, h):
            lines = [pl.ds(128 * i + 8 * h + k, 8, stride=16) for k in range(8)]
            tops = [mrun[p, :] for p in lines]
            top = functools.reduce(jnp.maximum, tops)
            return top + log2(sum(srun[p, :] * jnp.exp2(t - top) for p, t in zip(lines, tops)))

        lse = jnp.concatenate(
            [jnp.concatenate([over_sublanes(i, h) for h in (0, 1)], axis=1) for i in range(slots // 8)], axis=0
        )
        live = lax.broadcasted_iota(jnp.int32, (slots, 256), 0) < count
        lse = jnp.where(live, lse, -2000.0)
        gauge = dot(into[...], jnp.exp2(lse * (1.0 / SPREAD)).astype(jnp.bfloat16))
        level = (SPREAD * log2(gauge + TINY)).astype(jnp.bfloat16)
        scaled = jnp.exp2(lse - dot(back[...], level))
        coarse = scaled.astype(jnp.bfloat16)
        fine = (scaled - coarse.astype(jnp.float32)).astype(jnp.bfloat16)
        total = dot(into[...], coarse) + dot(into[...], fine)
        total = level.astype(jnp.float32) + log2(total + TINY)
        for h in (0, 1):
            part[h] = total[:, 128 * h : 128 * h + 128]

    def remote(src, dst, send, recv, peer):
        pltpu.make_async_remote_copy(
            src_ref=src, dst_ref=dst, send_sem=send, recv_sem=recv, device_id=peer, device_id_type=MESH
        ).start()

    def wait_bytes(ref, sem):
        pltpu.make_async_copy(ref, ref, sem).wait()

    def row_round(it, part, pot):
        rs, rr, gs, gr = rs_send.at[it, 0], rs_recv.at[it, 0], ag_send.at[it, 0], ag_recv.at[it, 0]
        inbox = rs_row.at[it]
        order = sorted(range(1, n_z), key=lambda d: -min(d, n_z - d))

        def share(owner):
            return pl.ds(pl.multiple_of(owner * r_rows, r_rows), r_rows)

        for d in order:
            remote(part.at[:, share((z + d) % n_z), :], inbox.at[t], rs, rr, row_hub(d))
        mine = pot.at[:, share(z), :]

        @pl.when(c == 0)
        def _():
            remote(part.at[:, share(z), :], inbox.at[t], rs, rr, (s, 2 * z + 1))
            wait_bytes(part, rs)
            wait_bytes(pot, gr)

        @pl.when(c == 1)
        def _():
            inbox[t] = part[:, share(z), :]
            wait_bytes(inbox.at[pl.ds(0, n_tgt - 1)], rr)
            mine[...] = blocks_of(la_v, r_rows) * LOG2E - lse2(inbox[...])
            for d in order:
                remote(mine, mine, gs, gr, row_low(d))
                remote(mine, mine, gs, gr, row_hub(d))
            remote(mine, mine, gs, gr, (s, 2 * z))
            wait_bytes(inbox.at[pl.ds(0, n_z - 1)], rs)
            wait_bytes(inbox.at[pl.ds(0, n_z - 1)], gr)
            wait_bytes(inbox.at[pl.ds(0, n_tgt - 1)], gs)

    def far(d):
        y, x = d // 4, d % 4
        return min(y, 4 - y) + min(x, 4 - x)

    def col_round(it, part, pot, last):
        rs, gr = rs_send.at[it, 1], ag_recv.at[it, 1]
        rr = rs_recv.at[it, 1 + c]
        rr_low, rr_high, gs_low, gs_high = [m.at[it, k] for m in (rs_recv, ag_send) for k in (1, 2)]
        inbox = rs_col.at[it]
        order = sorted(range(1, n_src), key=lambda d: -far(d))
        box = inbox.at[c, s]

        def share(owner):
            return part.at[:, pl.ds(pl.multiple_of(owner * c_rows, c_rows), c_rows), :]

        for d in order:
            remote(share((s + d) % n_src), box, rs, rr, col_hub(d))
        if last:
            home = pot.at[pl.ds(pl.multiple_of(s * 2 * c_rows, 2 * c_rows), 2 * c_rows)]
            own = [g_last.at[0], g_last.at[1]]
        else:
            home = pot.at[:, pl.ds(pl.multiple_of(s * c_rows, c_rows), c_rows), :]
            own = [g_own.at[0], g_own.at[1]]

        def settle(core, value):
            if last:
                for h in (0, 1):
                    own[core][pl.ds(h, c_rows, stride=2), :] = value[h] * LN2
            else:
                own[core][...] = value

        @pl.when(c == 0)
        def _():
            remote(share(s), box, rs, rr, (s, 2 * z + 1))
            wait_bytes(part, rs)
            wait_bytes(pot, gr)

        @pl.when(c == 1)
        def _():
            box[...] = share(s)[...]
            wait_bytes(inbox.at[0], rr_low)
            settle(0, blocks_of(lb_other, c_rows) * LOG2E - lse2(inbox[0]))
            for d in order:
                remote(own[0], home, gs_low, gr, col_low(d))
            remote(own[0], home, gs_low, gr, (s, 2 * z))
            wait_bytes(inbox.at[1, pl.ds(0, n_src - 1)], rr_high)
            settle(1, blocks_of(lb_v, c_rows) * LOG2E - lse2(inbox[1]))
            for d in order:
                remote(own[1], home, gs_high, gr, col_hub(d))
            keep = pltpu.make_async_copy(own[1], home, out_sem.at[1])
            keep.start()
            keep.wait()
            wait_bytes(inbox.at[1, pl.ds(0, n_src - 1)], rs)
            wait_bytes(inbox.at[1, pl.ds(0, n_src - 1)], gr)
            wait_bytes(inbox.at[0], gs_low)
            wait_bytes(inbox.at[1, pl.ds(0, n_src - 1)], gs_high)

    lax.fori_loop(0, n_chunks, prepare, 0)
    f_copy = pltpu.make_async_copy(f_nat, f_out, out_sem.at[0])
    for it in range(ITERS):
        sweep(kt, pots.at[2 * it], back_c, into_r, back_r, parts.at[2 * it])
        if it == 0:
            pl.semaphore_wait(barrier, jnp.where(c == 1, 2 * (n_z - 1) + 2 * (n_src - 1) + 1, n_z + n_src - 1))

            @pl.when(c == 0)
            def _():
                lb_remote = pltpu.make_async_remote_copy(
                    src_ref=lb_v, dst_ref=lb_other, send_sem=lb_sem, recv_sem=lb_rsem,
                    device_id=(s, 2 * z + 1), device_id_type=MESH,
                )
                lb_remote.start()
                lb_remote.wait_send()

        row_round(it, parts.at[2 * it], pots.at[2 * it + 1])
        if it == 0:
            @pl.when(c == 1)
            def _():
                wait_bytes(lb_other, lb_rsem)

        if it == ITERS - 1:
            for h in (0, 1):
                f_nat[pl.ds(h, 128, stride=2), :] = pots[2 * it + 1, h] * LN2
            f_copy.start()
        sweep(kf, pots.at[2 * it + 1], back_r, into_c, back_c, parts.at[2 * it + 1])
        last = it == ITERS - 1
        col_round(it, parts.at[2 * it + 1], g_out if last else pots.at[2 * it + 2], last)
    f_copy.wait()


def hand_over(f_in, g_in, f_out, g_out):
    f_out[...] = f_in[...]
    g_out[...] = g_in[...]


def per_device(n_src, n_tgt, log_kernel, tile_rows, tile_cols, tile_count, log_a, log_b, g_start):
    slots, width = log_kernel.shape[2], log_kernel.shape[3]
    f32 = jnp.float32
    anywhere = pl.BlockSpec(memory_space=pl.ANY)
    vmem = pl.BlockSpec(memory_space=pltpu.VMEM)
    smem = pl.BlockSpec(memory_space=pltpu.SMEM)
    r_rows, c_rows = 128 // (n_tgt // 2), 128 // n_src
    dma = pltpu.SemaphoreType.DMA
    f, g = pl.pallas_call(
        functools.partial(whole, n_src, n_tgt),
        out_shape=(jax.ShapeDtypeStruct((256, 128), f32), jax.ShapeDtypeStruct((256, 128), f32)),
        in_specs=[anywhere, vmem, vmem, smem, anywhere, anywhere, anywhere],
        out_specs=(anywhere, anywhere),
        scratch_shapes=[
            pltpu.VMEM((slots, width, width), jnp.bfloat16),
            pltpu.VMEM((slots, width, width), f32),
            pltpu.VMEM((slots, width, width), f32),
            pltpu.VMEM((2 * ITERS, 2, 128, 128), f32),
            pltpu.VMEM((2 * ITERS, 2, 128, 128), f32),
            pltpu.VMEM((ITERS, n_tgt, 2, r_rows, 128), f32),
            pltpu.VMEM((ITERS, 2, n_src, 2, c_rows, 128), f32),
            pltpu.VMEM((2 * r_rows, 128), f32),
            pltpu.VMEM((2 * c_rows, 128), f32),
            pltpu.VMEM((2 * c_rows, 128), f32),
            pltpu.VMEM((2, 2, c_rows, 128), f32),
            pltpu.VMEM((2, 2 * c_rows, 128), f32),
            pltpu.VMEM((256, 128), f32),
            pltpu.VMEM((2 * slots, 128), f32),
            pltpu.VMEM((GROUP, 256, 128), f32),
            pltpu.VMEM((GROUP, 256, 128), f32),
            pltpu.VMEM((16 * slots + 8, 128), f32),
            pltpu.VMEM((16 * slots, 128), f32),
            pltpu.VMEM((256, 128), f32),
            pltpu.VMEM((128, slots), jnp.bfloat16),
            pltpu.VMEM((slots, 128), jnp.bfloat16),
            pltpu.VMEM((128, slots), jnp.bfloat16),
            pltpu.VMEM((slots, 128), jnp.bfloat16),
            dma((slots // CHUNK,)),
            dma((3,)),
            dma((2,)),
            dma,
            dma,
            dma((ITERS, 2)),
            dma((ITERS, 3)),
            dma((ITERS, 3)),
            dma((ITERS, 2)),
        ],
        compiler_params=pltpu.CompilerParams(
            collective_id=0, has_side_effects=True, vmem_limit_bytes=56 * 1024 * 1024
        ),
        name="sinkhorn",
    )(
        log_kernel.reshape(slots, width, width),
        tile_rows.reshape(1, slots),
        tile_cols.reshape(1, slots),
        tile_count,
        log_a.reshape(256, 128),
        log_b.reshape(256, 128),
        g_start.reshape(256, 128),
    )
    f, g = pl.pallas_call(
        hand_over,
        out_shape=(jax.ShapeDtypeStruct((256, 128), f32), jax.ShapeDtypeStruct((256, 128), f32)),
        in_specs=[vmem, vmem],
        out_specs=(vmem, vmem),
        name="hand_over",
    )(f, g)
    return f.reshape(-1), g.reshape(-1)


def solution(mesh):
    n_src, n_tgt = mesh.shape["src"], mesh.shape["tgt"]
    in_specs = (
        P("src", "tgt", None, None, None),
        P("src", "tgt", None),
        P("src", "tgt", None),
        P("src", "tgt"),
        P("src"),
        P("tgt"),
        P("tgt"),
    )
    return jax.shard_map(
        functools.partial(per_device, n_src, n_tgt),
        mesh=mesh, in_specs=in_specs, out_specs=(P("src"), P("tgt")), check_vma=False,
    )
```

```python
import functools

import jax
import jax.numpy as jnp
from jax import lax
from jax.experimental import pallas as pl
from jax.experimental.pallas import tpu as pltpu
from jax.sharding import PartitionSpec as P

ITERS = 2
TINY = 1e-37
LOG2E = 1.4426950408889634
LN2 = 0.6931471805599453
MESH = pl.DeviceIdType.MESH
GROUP = 4
CHUNK = 4

SPREAD = 8.0


def lse2(values):
    top = jnp.max(values, axis=0)
    total = jnp.sum(jnp.exp2(values - top[None]), axis=0)
    return top + log2(total)


def membership(ids_ref, count, into, back):
    slots = ids_ref.shape[1]
    block = lax.broadcasted_iota(jnp.int32, (128, slots), 0)
    slot = lax.broadcasted_iota(jnp.int32, (128, slots), 1)
    hit = (ids_ref[...] == block) & (slot < count)
    hit = jnp.where(hit, 1.0, 0.0)
    into[...] = hit.astype(jnp.bfloat16)
    back[...] = hit.T.astype(jnp.bfloat16)


def dot(a, b):
    return jnp.dot(a, b, preferred_element_type=jnp.float32)


def log2(x):
    return jnp.log(x) * LOG2E


def whole(
    n_src, n_tgt,
    k_hbm, rows_hbm, cols_hbm, count_ref, la_hbm, lb_hbm, g0_hbm,
    f_out, g_out,
    rows_ref, cols_ref, kb, kt, kf, pots, parts, rs_row, rs_col, la_v, lb_v, lb_low, g_low, g_last, g_raw, gathered, wide0, wide1,
    kept, mrun, srun, into_r, back_r, into_c, back_c,
    k_sem, in_sem, out_sem, lb_sem, lb_rsem, rs_send, rs_recv, ag_send, ag_recv,
):
    s, t = lax.axis_index("src"), lax.axis_index("tgt")
    z, c = t // 2, t % 2
    slots = kb.shape[0]
    n_chunks = slots // CHUNK
    n_z = n_tgt // 2
    r_rows = 128 // n_z
    c_rows = 128 // n_src
    low_core = (s, 2 * z)
    hub = (s, 2 * z + 1)

    def k_copy(i):
        piece = pl.ds(i * CHUNK, CHUNK)
        return pltpu.make_async_copy(k_hbm.at[piece], kb.at[piece], k_sem.at[i])

    g0_copy = pltpu.make_async_copy(g0_hbm, g_raw, in_sem.at[0])
    g0_copy.start()
    for i in range(n_chunks):
        k_copy(i).start()
    id_copies = [
        pltpu.make_async_copy(rows_hbm, rows_ref, in_sem.at[3]),
        pltpu.make_async_copy(cols_hbm, cols_ref, in_sem.at[4]),
    ]
    for copy in id_copies:
        copy.start()
    la_copy = pltpu.make_async_copy(la_hbm.at[pl.ds(2 * z * r_rows, 2 * r_rows)], la_v, in_sem.at[1])
    la_copy.start()
    lb_copy = pltpu.make_async_copy(lb_hbm.at[pl.ds(2 * s * c_rows, 2 * c_rows)], lb_v, in_sem.at[2])
    lb_copy.start()

    def row_hub(d):
        return (s, 2 * ((z + d) % n_z) + 1)

    def row_low(d):
        return (s, 2 * ((z + d) % n_z))

    def col_hub(d):
        return ((s + d) % n_src, 2 * z + 1)

    def col_low(d):
        return ((s + d) % n_src, 2 * z)

    barrier = pltpu.get_barrier_semaphore()

    def greet(peer):
        pl.semaphore_signal(barrier, inc=1, device_id=peer, device_id_type=MESH)

    @pl.when(c == 1)
    def _():
        for d in range(1, n_z):
            greet(row_hub(d))
            greet(row_low(d))
        for d in range(1, n_src):
            greet(col_hub(d))
            greet(col_low(d))
        greet(low_core)

    @pl.when(c == 0)
    def _():
        for d in range(1, n_z):
            greet(row_hub(d))
        for d in range(1, n_src):
            greet(col_hub(d))
        greet(hub)

    for copy in id_copies:
        copy.wait()
    count = count_ref[0, 0]
    membership(rows_ref, count, into_r, back_r)
    membership(cols_ref, count, into_c, back_c)

    def blocks_of(ref, rows, h):
        return ref[pl.ds(h, rows, stride=2), :]

    g0_copy.wait()
    for h in (0, 1):
        pots[0, h] = blocks_of(g_raw, 128, h) * LOG2E

    def flip_tiles(i, carry):
        k_copy(i).wait()
        for u in range(CHUNK):
            slot = i * CHUNK + u
            for p in (0, 1):
                for q in (0, 1):
                    piece = kb[slot, 128 * p : 128 * p + 128, 128 * q : 128 * q + 128]
                    flipped = piece.T.astype(jnp.float32) * LOG2E
                    kt[slot, 128 * q : 128 * q + 128, 128 * p : 128 * p + 128] = flipped
        return carry

    def widen_tiles(i, carry):
        for u in range(CHUNK):
            kf[i * CHUNK + u] = kb[i * CHUNK + u].astype(jnp.float32) * LOG2E
        return carry

    def gather(pot, pick):
        value = pot[...]
        rows = jnp.zeros((slots, 128), jnp.float32)
        for _ in range(3):
            piece = value.astype(jnp.bfloat16)
            rows += dot(pick[...], piece)
            value -= piece.astype(jnp.float32)
        gathered[...] = rows

    def spread(wide, slot, keep):
        for u in range(GROUP):
            at = jnp.minimum(slot + u, slots - 1)
            row = jnp.broadcast_to(gathered[pl.ds(at, 1), :], (128, 128)).T
            wide[u] = row
            if keep:
                kept[at] = row

    def add_up(tiles, wide, first, slot, q, halves, guard):
        for u in range(GROUP):
            for h in halves:
                x = tiles[slot + u, 128 * q : 128 * q + 128, 128 * h : 128 * h + 128] + wide[first + u]
                x = x.reshape(16, 8, 128)
                here = pl.ds(pl.multiple_of((slot + u) * 16 + 8 * h, 8), 8)
                old = mrun[guard if q == 0 else here, :]
                top = jnp.maximum(jnp.max(x, axis=0), old)
                mrun[here, :] = top
                total = jnp.sum(jnp.exp2(x - top[None]), axis=0)
                if q == 1:
                    total += srun[here, :] * jnp.exp2(old - top)
                srun[here, :] = total

    def sweep(tiles, q, halves, keep):
        def step(i, carry):
            slot = i * (2 * GROUP)
            guard = pl.ds(pl.multiple_of(16 * slots + 8 * jnp.maximum(i - slots, 0), 8), 8)
            spread(wide1, slot + GROUP, keep)
            add_up(tiles, wide0, 0, slot, q, halves, guard)
            spread(wide0, slot + 2 * GROUP, keep)
            add_up(tiles, wide1, 0, slot + GROUP, q, halves, guard)
            return carry

        spread(wide0, 0, keep)
        lax.fori_loop(0, slots // (2 * GROUP), step, 0)

    def sweep_kept(tiles, q, halves):
        def step(i, carry):
            slot = i * (2 * GROUP)
            add_up(tiles, kept, slot, slot, q, halves, None)
            add_up(tiles, kept, slot + GROUP, slot + GROUP, q, halves, None)
            return carry

        lax.fori_loop(0, slots // (2 * GROUP), step, 0)

    def fold(h, into, back, part):
        def over_sublanes(i):
            lines = [pl.ds(128 * i + 8 * h + k, 8, stride=16) for k in range(8)]
            tops = [mrun[p, :] for p in lines]
            top = functools.reduce(jnp.maximum, tops)
            return top + log2(sum(srun[p, :] * jnp.exp2(m - top) for p, m in zip(lines, tops)))

        lse = jnp.concatenate([over_sublanes(i) for i in range(slots // 8)], axis=0)
        live = lax.broadcasted_iota(jnp.int32, (slots, 128), 0) < count
        lse = jnp.where(live, lse, -2000.0)
        gauge = dot(into[...], jnp.exp2(lse * (1.0 / SPREAD)).astype(jnp.bfloat16))
        level = (SPREAD * log2(gauge + TINY)).astype(jnp.bfloat16)
        scaled = jnp.exp2(lse - dot(back[...], level))
        coarse = scaled.astype(jnp.bfloat16)
        fine = (scaled - coarse.astype(jnp.float32)).astype(jnp.bfloat16)
        total = dot(into[...], coarse) + dot(into[...], fine)
        part[...] = level.astype(jnp.float32) + log2(total + TINY)

    def remote(src, dst, send, recv, peer):
        pltpu.make_async_remote_copy(
            src_ref=src, dst_ref=dst, send_sem=send, recv_sem=recv, device_id=peer, device_id_type=MESH
        ).start()

    def wait_bytes(ref, sem):
        pltpu.make_async_copy(ref, ref, sem).wait()

    def far(d):
        y, x = d // 4, d % 4
        return min(y, 4 - y) + min(x, 4 - x)

    row_order = sorted(range(1, n_z), key=lambda d: -min(d, n_z - d))
    col_order = sorted(range(1, n_src), key=lambda d: -far(d))

    def row_share(ref, owner):
        return ref.at[pl.ds(pl.multiple_of(owner * r_rows, r_rows), r_rows), :]

    def col_share(ref, owner):
        return ref.at[pl.ds(pl.multiple_of(owner * c_rows, c_rows), c_rows), :]

    def send_rows(it, h):
        part, box = parts.at[2 * it, h], rs_row.at[it, h, t]
        sems = rs_send.at[2 * it, h], rs_recv.at[2 * it, h, 0]
        for d in row_order:
            remote(row_share(part, (z + d) % n_z), box, *sems, row_hub(d))

        @pl.when(c == 0)
        def _():
            remote(row_share(part, z), box, *sems, hub)

        @pl.when(c == 1)
        def _():
            box[...] = row_share(part, z)[...]

    def settle_rows(it):
        @pl.when(c == 1)
        def _():
            for h in (0, 1):
                inbox = rs_row.at[it, h]
                mine = row_share(pots.at[2 * it + 1, h], z)
                sems = ag_send.at[2 * it, h, 0], ag_recv.at[2 * it, h]
                wait_bytes(inbox.at[pl.ds(0, n_tgt - 1)], rs_recv.at[2 * it, h, 0])
                mine[...] = blocks_of(la_v, r_rows, h) * LOG2E - lse2(inbox[...])
                for d in row_order:
                    remote(mine, mine, *sems, row_low(d))
                    remote(mine, mine, *sems, row_hub(d))
                remote(mine, mine, *sems, low_core)

    def wait_rows(it, h):
        pot, sem = pots.at[2 * it + 1, h], ag_recv.at[2 * it, h]

        @pl.when(c == 0)
        def _():
            wait_bytes(pot, sem)

        @pl.when(c == 1)
        def _():
            wait_bytes(pot.at[pl.ds(0, (n_z - 1) * r_rows)], sem)

    def send_cols(it, h):
        part, box = parts.at[2 * it + 1, h], rs_col.at[it, h, c, s]
        sems = rs_send.at[2 * it + 1, h], rs_recv.at[2 * it + 1, h, c]
        for d in col_order:
            remote(col_share(part, (s + d) % n_src), box, *sems, col_hub(d))

        @pl.when(c == 0)
        def _():
            remote(col_share(part, s), box, *sems, hub)

        @pl.when(c == 1)
        def _():
            box[...] = col_share(part, s)[...]

    def reduced(it, h, core):
        inbox = rs_col.at[it, h, core]
        sem = rs_recv.at[2 * it + 1, h, core]
        wait_bytes(inbox.at[pl.ds(0, n_src - core)], sem)
        return blocks_of((lb_low, lb_v)[core], c_rows, h) * LOG2E - lse2(inbox[...])

    def settle_cols(it):
        @pl.when(c == 1)
        def _():
            for h in (0, 1):
                there = col_share(pots.at[2 * it + 2, h], s)
                recv = ag_recv.at[2 * it + 1, h]
                low = g_low.at[it, h]
                low[...] = reduced(it, h, 0)
                for d in col_order:
                    remote(low, there, ag_send.at[2 * it + 1, h, 0], recv, col_low(d))
                remote(low, there, ag_send.at[2 * it + 1, h, 0], recv, low_core)
                there[...] = reduced(it, h, 1)
                for d in col_order:
                    remote(there, there, ag_send.at[2 * it + 1, h, 1], recv, col_hub(d))

    def wait_cols(it, h):
        pot, sem = pots.at[2 * it + 2, h], ag_recv.at[2 * it + 1, h]

        @pl.when(c == 0)
        def _():
            wait_bytes(pot, sem)

        @pl.when(c == 1)
        def _():
            wait_bytes(pot.at[pl.ds(0, (n_src - 1) * c_rows)], sem)

    def last_cols(it):
        home = g_out.at[pl.ds(pl.multiple_of(s * 2 * c_rows, 2 * c_rows), 2 * c_rows)]
        recv = ag_recv.at[2 * it + 1, 0]

        @pl.when(c == 1)
        def _():
            for core in (0, 1):
                for h in (0, 1):
                    g_last[core, pl.ds(h, c_rows, stride=2), :] = reduced(it, h, core) * LN2
                send = ag_send.at[2 * it + 1, 0, core]
                for d in col_order:
                    remote(g_last.at[core], home, send, recv, (col_low, col_hub)[core](d))
                if core == 0:
                    remote(g_last.at[0], home, send, recv, low_core)
            keep = pltpu.make_async_copy(g_last.at[1], home, out_sem)
            keep.start()
            keep.wait()
            wait_bytes(g_out.at[pl.ds(0, (n_src - 1) * 2 * c_rows)], recv)

        @pl.when(c == 0)
        def _():
            wait_bytes(g_out, recv)

    mrun[16 * slots : 16 * slots + 8, :] = jnp.full((8, 128), -1e30, jnp.float32)
    lax.fori_loop(0, n_chunks, flip_tiles, 0)
    for it in range(ITERS):
        gather(pots.at[2 * it, 0], back_c) if it == 0 else None
        for q in (0, 1):
            if it > 0:
                wait_cols(it - 1, q)
                gather(pots.at[2 * it, q], back_c)
            elif q == 1:
                gather(pots.at[2 * it, q], back_c)
            sweep(kt, q, (0, 1) if q == 0 else (0,), q == 1)
        fold(0, into_r, back_r, parts.at[2 * it, 0])
        if it == 0:
            pl.semaphore_wait(barrier, jnp.where(c == 1, 2 * (n_z - 1) + 2 * (n_src - 1) + 1, n_z + n_src - 1))
        send_rows(it, 0)
        sweep_kept(kt, 1, (1,))
        fold(1, into_r, back_r, parts.at[2 * it, 1])
        send_rows(it, 1)
        if it == 0:
            la_copy.wait()
            lb_copy.wait()

            @pl.when(c == 0)
            def _():
                remote(lb_v, lb_low, lb_sem, lb_rsem, hub)

            lax.fori_loop(0, n_chunks, widen_tiles, 0)
        settle_rows(it)
        for q in (0, 1):
            wait_rows(it, q)
            gather(pots.at[2 * it + 1, q], back_r)
            sweep(kf, q, (0, 1) if q == 0 else (0,), q == 1)
        fold(0, into_c, back_c, parts.at[2 * it + 1, 0])
        send_cols(it, 0)
        sweep_kept(kf, 1, (1,))
        fold(1, into_c, back_c, parts.at[2 * it + 1, 1])
        send_cols(it, 1)
        if it == 0:
            @pl.when(c == 1)
            def _():
                wait_bytes(lb_low, lb_rsem)

        if it < ITERS - 1:
            settle_cols(it)
    for h in (0, 1):
        f_out[pl.ds(h, 128, stride=2), :] = pots[2 * ITERS - 1, h] * LN2
    last_cols(ITERS - 1)

    for k in range(2 * ITERS):
        for h in (0, 1):
            part, sem = parts.at[k, h], rs_send.at[k, h]
            own_rows = r_rows if k % 2 == 0 else c_rows

            @pl.when(c == 0)
            def _():
                wait_bytes(part, sem)

            @pl.when(c == 1)
            def _():
                wait_bytes(part.at[pl.ds(0, 128 - own_rows)], sem)
                if k % 2 == 0:
                    wait_bytes(rs_row.at[0, 0, pl.ds(0, n_tgt - 1)], ag_send.at[k, h, 0])
                elif k < 2 * ITERS - 1:
                    wait_bytes(rs_col.at[0, 0, 0], ag_send.at[k, h, 0])
                    wait_bytes(rs_col.at[0, 0, 0, pl.ds(0, n_src - 1)], ag_send.at[k, h, 1])
                elif h == 0:
                    wait_bytes(g_out, ag_send.at[k, h, 0])
                    wait_bytes(g_out.at[pl.ds(0, (n_src - 1) * 2 * c_rows)], ag_send.at[k, h, 1])

    @pl.when(c == 0)
    def _():
        wait_bytes(lb_v, lb_sem)


def per_device(n_src, n_tgt, log_kernel, tile_rows, tile_cols, tile_count, log_a, log_b, g_start):
    slots, width = log_kernel.shape[2], log_kernel.shape[3]
    f32 = jnp.float32
    anywhere = pl.BlockSpec(memory_space=pl.ANY)
    vmem = pl.BlockSpec(memory_space=pltpu.VMEM)
    smem = pl.BlockSpec(memory_space=pltpu.SMEM)
    r_rows, c_rows = 128 // (n_tgt // 2), 128 // n_src
    dma = pltpu.SemaphoreType.DMA
    f, g = pl.pallas_call(
        functools.partial(whole, n_src, n_tgt),
        out_shape=(pltpu.VMEM((256, 128), f32), pltpu.VMEM((256, 128), f32)),
        in_specs=[anywhere, anywhere, anywhere, smem, anywhere, anywhere, anywhere],
        out_specs=(vmem, vmem),
        scratch_shapes=[
            pltpu.VMEM((1, slots), jnp.int32),
            pltpu.VMEM((1, slots), jnp.int32),
            pltpu.VMEM((slots, width, width), jnp.bfloat16),
            pltpu.VMEM((slots, width, width), f32),
            pltpu.VMEM((slots, width, width), f32),
            pltpu.VMEM((2 * ITERS, 2, 128, 128), f32),
            pltpu.VMEM((2 * ITERS, 2, 128, 128), f32),
            pltpu.VMEM((ITERS, 2, n_tgt, r_rows, 128), f32),
            pltpu.VMEM((ITERS, 2, 2, n_src, c_rows, 128), f32),
            pltpu.VMEM((2 * r_rows, 128), f32),
            pltpu.VMEM((2 * c_rows, 128), f32),
            pltpu.VMEM((2 * c_rows, 128), f32),
            pltpu.VMEM((ITERS, 2, c_rows, 128), f32),
            pltpu.VMEM((2, 2 * c_rows, 128), f32),
            pltpu.VMEM((256, 128), f32),
            pltpu.VMEM((slots, 128), f32),
            pltpu.VMEM((GROUP, 128, 128), f32),
            pltpu.VMEM((GROUP, 128, 128), f32),
            pltpu.VMEM((slots, 128, 128), f32),
            pltpu.VMEM((16 * slots + 8, 128), f32),
            pltpu.VMEM((16 * slots, 128), f32),
            pltpu.VMEM((128, slots), jnp.bfloat16),
            pltpu.VMEM((slots, 128), jnp.bfloat16),
            pltpu.VMEM((128, slots), jnp.bfloat16),
            pltpu.VMEM((slots, 128), jnp.bfloat16),
            dma((slots // CHUNK,)),
            dma((5,)),
            dma,
            dma,
            dma,
            dma((2 * ITERS, 2)),
            dma((2 * ITERS, 2, 2)),
            dma((2 * ITERS, 2, 2)),
            dma((2 * ITERS, 2)),
        ],
        compiler_params=pltpu.CompilerParams(
            collective_id=0, has_side_effects=True, vmem_limit_bytes=56 * 1024 * 1024
        ),
        name="sinkhorn",
    )(
        log_kernel.reshape(slots, width, width),
        tile_rows.reshape(1, slots),
        tile_cols.reshape(1, slots),
        tile_count,
        log_a.reshape(256, 128),
        log_b.reshape(256, 128),
        g_start.reshape(256, 128),
    )
    return f.reshape(-1), g.reshape(-1)


def solution(mesh):
    n_src, n_tgt = mesh.shape["src"], mesh.shape["tgt"]
    in_specs = (
        P("src", "tgt", None, None, None),
        P("src", "tgt", None),
        P("src", "tgt", None),
        P("src", "tgt"),
        P("src"),
        P("tgt"),
        P("tgt"),
    )
    return jax.shard_map(
        functools.partial(per_device, n_src, n_tgt),
        mesh=mesh, in_specs=in_specs, out_specs=(P("src"), P("tgt")), check_vma=False,
    )
```

```python
import functools

import jax
import jax.numpy as jnp
from jax import lax
from jax.experimental import pallas as pl
from jax.experimental.pallas import tpu as pltpu
from jax.sharding import PartitionSpec as P

ITERS = 2
TINY = 1e-37
LOG2E = 1.4426950408889634
LN2 = 0.6931471805599453
MESH = pl.DeviceIdType.MESH
GROUP = 6
CHUNK = 4

SPREAD = 8.0


def lse2(values):
    top = jnp.max(values, axis=0)
    total = jnp.sum(jnp.exp2(values - top[None]), axis=0)
    return top + log2(total)


def membership(ids_ref, count, into, back):
    slots = ids_ref.shape[1]
    block = lax.broadcasted_iota(jnp.int32, (128, slots), 0)
    slot = lax.broadcasted_iota(jnp.int32, (128, slots), 1)
    hit = (ids_ref[...] == block) & (slot < count)
    hit = jnp.where(hit, 1.0, 0.0)
    into[...] = hit.astype(jnp.bfloat16)
    back[...] = hit.T.astype(jnp.bfloat16)


def dot(a, b):
    return jnp.dot(a, b, preferred_element_type=jnp.float32)


def log2(x):
    return jnp.log(x) * LOG2E


def whole(
    n_src, n_tgt,
    k_hbm, rows_hbm, cols_hbm, count_ref, la_hbm, lb_hbm, g0_hbm,
    f_out, g_out,
    rows_ref, cols_ref, kb, kt, kf, pots, parts, rs_row, rs_col, la_v, lb_v, lb_low, g_low, g_last, g_raw, gathered, wide0, wide1,
    kept0, kept, mrun, srun, into_r, back_r, into_c, back_c,
    k_sem, in_sem, out_sem, lb_sem, lb_rsem, rs_send, rs_recv, ag_send, ag_recv,
):
    s, t = lax.axis_index("src"), lax.axis_index("tgt")
    z, c = t // 2, t % 2
    slots = kb.shape[0]
    n_chunks = slots // CHUNK
    n_z = n_tgt // 2
    r_shares, c_shares = n_z, n_src // 2
    r_rows, c_rows = 128 // r_shares, 128 // c_shares
    side = 4
    y, x = s // side, s % side

    def col_share_of(y, x):
        return (y % 2) * side + (x + 2 * (y // 2)) % side

    r_mine, c_mine = z % r_shares, col_share_of(y, x)
    low_core = (s, 2 * z)
    hub = (s, 2 * z + 1)

    def k_copy(i):
        piece = pl.ds(i * CHUNK, CHUNK)
        return pltpu.make_async_copy(k_hbm.at[piece], kb.at[piece], k_sem.at[i])

    g0_copy = pltpu.make_async_copy(g0_hbm, g_raw, in_sem.at[0])
    g0_copy.start()
    for i in range(n_chunks):
        k_copy(i).start()
    id_copies = [
        pltpu.make_async_copy(rows_hbm, rows_ref, in_sem.at[3]),
        pltpu.make_async_copy(cols_hbm, cols_ref, in_sem.at[4]),
    ]
    for copy in id_copies:
        copy.start()
    la_copy = pltpu.make_async_copy(la_hbm.at[pl.ds(2 * r_mine * r_rows, 2 * r_rows)], la_v, in_sem.at[1])
    la_copy.start()
    lb_copy = pltpu.make_async_copy(lb_hbm.at[pl.ds(2 * c_mine * c_rows, 2 * c_rows)], lb_v, in_sem.at[2])
    lb_copy.start()

    def row_hub(d):
        return (s, 2 * ((z + d) % n_z) + 1)

    def row_low(d):
        return (s, 2 * ((z + d) % n_z))

    def torus(d):
        return (y + d[0]) % side, (x + d[1]) % side

    def col_hub(d):
        return (torus(d)[0] * side + torus(d)[1], 2 * z + 1)

    def col_low(d):
        return (torus(d)[0] * side + torus(d)[1], 2 * z)

    def around(d):
        return min(d, side - d)

    row_order = sorted(range(1, n_z), key=lambda d: -min(d, n_z - d))
    row_near = row_order
    col_order = [(dy, dx) for dy in range(side) for dx in range(side) if dy or dx]
    col_order.sort(key=lambda d: -around(d[0]) - around(d[1]))
    col_near = ((0, 2), (1, 1), (1, 3), (0, 1), (0, 3), (1, 0), (3, 0))

    barrier = pltpu.get_barrier_semaphore()

    def greet(peer):
        pl.semaphore_signal(barrier, inc=1, device_id=peer, device_id_type=MESH)

    @pl.when(c == 1)
    def _():
        for d in range(1, n_z):
            greet(row_hub(d))
            greet(row_low(d))
        for d in col_order:
            greet(col_hub(d))
            greet(col_low(d))
        greet(low_core)

    @pl.when(c == 0)
    def _():
        for d in range(1, n_z):
            greet(row_hub(d))
        for d in col_order:
            greet(col_hub(d))
        greet(hub)

    for copy in id_copies:
        copy.wait()
    count = count_ref[0, 0]
    membership(rows_ref, count, into_r, back_r)
    membership(cols_ref, count, into_c, back_c)

    def blocks_of(ref, rows, h):
        return ref[pl.ds(h, rows, stride=2), :]

    g0_copy.wait()
    for h in (0, 1):
        pots[0, h] = blocks_of(g_raw, 128, h) * LOG2E

    def flip(slot):
        for p in (0, 1):
            for q in (0, 1):
                piece = kb[slot, 128 * p : 128 * p + 128, 128 * q : 128 * q + 128]
                flipped = piece.T.astype(jnp.float32) * LOG2E
                kt[slot, 128 * q : 128 * q + 128, 128 * p : 128 * p + 128] = flipped

    def widen_tiles(i, carry):
        for u in range(CHUNK):
            kf[i * CHUNK + u] = kb[i * CHUNK + u].astype(jnp.float32) * LOG2E
        return carry

    def gather(pot, pick, q):
        value = pot[...]
        rows = jnp.zeros((slots, 128), jnp.float32)
        for _ in range(3):
            piece = value.astype(jnp.bfloat16)
            rows += dot(pick[...], piece)
            value -= piece.astype(jnp.float32)
        gathered[q] = rows

    def spread(q, slot, *places):
        row = jnp.broadcast_to(gathered[q, pl.ds(slot, 1), :], (128, 128)).T
        for wide, u in places:
            wide[u] = row

    def add_up(tiles, wide, u, slot, q, halves, guard):
        for h in halves:
            x = tiles[slot, 128 * q : 128 * q + 128, 128 * h : 128 * h + 128] + wide[u]
            x = x.reshape(16, 8, 128)
            here = pl.ds(pl.multiple_of(slot * 16 + 8 * h, 8), 8)
            old = mrun[guard if q == 0 else here, :]
            top = jnp.maximum(jnp.max(x, axis=0), old)
            mrun[here, :] = top
            total = jnp.sum(jnp.exp2(x - top[None]), axis=0)
            if q == 1:
                total += srun[here, :] * jnp.exp2(old - top)
            srun[here, :] = total

    def guard_of(i):
        return pl.ds(pl.multiple_of(16 * slots + 8 * jnp.maximum(i - slots, 0), 8), 8)

    def sweep(tiles, q, halves, keep):
        def ahead(wide, u, slot):
            at = jnp.minimum(slot, slots - 1)
            spread(q, at, (wide, u), *([(kept, at)] if keep else []))

        def step(i, carry):
            slot = i * (2 * GROUP)
            guard = guard_of(i)
            for u in range(GROUP):
                add_up(tiles, wide0, u, slot + u, q, halves, guard)
                ahead(wide1, u, slot + GROUP + u)
            for u in range(GROUP):
                add_up(tiles, wide1, u, slot + GROUP + u, q, halves, guard)
                ahead(wide0, u, slot + 2 * GROUP + u)
            return carry

        for u in range(GROUP):
            ahead(wide0, u, u)
        lax.fori_loop(0, slots // (2 * GROUP), step, 0)

    def first_sweep():
        def ahead(slot):
            flip(slot)
            spread(0, slot, (kept0, slot))
            spread(1, slot, (kept, slot))

        def add(i, u):
            slot = i * CHUNK + u
            add_up(kt, kept0, slot, slot, 0, (0, 1), guard_of(i))
            add_up(kt, kept, slot, slot, 1, (0,), None)

        def step(i, carry):
            k_copy(i + 1).wait()
            for u in range(CHUNK):
                add(i, u)
                ahead((i + 1) * CHUNK + u)
            return carry

        k_copy(0).wait()
        for u in range(CHUNK):
            ahead(u)
        lax.fori_loop(0, n_chunks - 1, step, 0)
        for u in range(CHUNK):
            add(n_chunks - 1, u)

    def sweep_kept(tiles, q, halves):
        def step(i, carry):
            for u in range(2 * GROUP):
                slot = i * (2 * GROUP) + u
                add_up(tiles, kept, slot, slot, q, halves, None)
            return carry

        lax.fori_loop(0, slots // (2 * GROUP), step, 0)

    def fold(h, into, back, part):
        def over_sublanes(i):
            lines = [pl.ds(128 * i + 8 * h + k, 8, stride=16) for k in range(8)]
            tops = [mrun[p, :] for p in lines]
            top = functools.reduce(jnp.maximum, tops)
            return top + log2(sum(srun[p, :] * jnp.exp2(m - top) for p, m in zip(lines, tops)))

        lse = jnp.concatenate([over_sublanes(i) for i in range(slots // 8)], axis=0)
        live = lax.broadcasted_iota(jnp.int32, (slots, 128), 0) < count
        lse = jnp.where(live, lse, -2000.0)
        gauge = dot(into[...], jnp.exp2(lse * (1.0 / SPREAD)).astype(jnp.bfloat16))
        level = (SPREAD * log2(gauge + TINY)).astype(jnp.bfloat16)
        scaled = jnp.exp2(lse - dot(back[...], level))
        coarse = scaled.astype(jnp.bfloat16)
        fine = (scaled - coarse.astype(jnp.float32)).astype(jnp.bfloat16)
        total = dot(into[...], coarse) + dot(into[...], fine)
        part[...] = level.astype(jnp.float32) + log2(total + TINY)

    def remote(src, dst, send, recv, peer):
        pltpu.make_async_remote_copy(
            src_ref=src, dst_ref=dst, send_sem=send, recv_sem=recv, device_id=peer, device_id_type=MESH
        ).start()

    def wait_bytes(ref, sem):
        pltpu.make_async_copy(ref, ref, sem).wait()

    def row_share(ref, owner):
        return ref.at[pl.ds(pl.multiple_of(owner * r_rows, r_rows), r_rows), :]

    def col_share(ref, owner):
        return ref.at[pl.ds(pl.multiple_of(owner * c_rows, c_rows), c_rows), :]

    def send_rows(it, h):
        part, box = parts.at[2 * it, h], rs_row.at[it, h, t]
        sems = rs_send.at[2 * it, h], rs_recv.at[2 * it, h, 0]
        for d in row_order:
            remote(row_share(part, (z + d) % r_shares), box, *sems, row_hub(d))

        @pl.when(c == 0)
        def _():
            remote(row_share(part, r_mine), box, *sems, hub)

        @pl.when(c == 1)
        def _():
            box[...] = row_share(part, r_mine)[...]

    def settle_rows(it):
        @pl.when(c == 1)
        def _():
            for h in (0, 1):
                inbox = rs_row.at[it, h]
                mine = row_share(pots.at[2 * it + 1, h], r_mine)
                sems = ag_send.at[2 * it, h, 0], ag_recv.at[2 * it, h]
                wait_bytes(inbox.at[pl.ds(0, n_tgt - 1)], rs_recv.at[2 * it, h, 0])
                mine[...] = blocks_of(la_v, r_rows, h) * LOG2E - lse2(inbox[...])
                for d in row_near:
                    remote(mine, mine, *sems, row_low(d))
                    remote(mine, mine, *sems, row_hub(d))
                remote(mine, mine, *sems, low_core)

    def wait_rows(it, h):
        pot, sem = pots.at[2 * it + 1, h], ag_recv.at[2 * it, h]

        @pl.when(c == 0)
        def _():
            wait_bytes(pot, sem)

        @pl.when(c == 1)
        def _():
            wait_bytes(pot.at[pl.ds(0, 128 - r_rows)], sem)

    def send_cols(it, h):
        part, box = parts.at[2 * it + 1, h], rs_col.at[it, h, c, s]
        sems = rs_send.at[2 * it + 1, h], rs_recv.at[2 * it + 1, h, c]
        for d in col_order:
            remote(col_share(part, col_share_of(*torus(d))), box, *sems, col_hub(d))

        @pl.when(c == 0)
        def _():
            remote(col_share(part, c_mine), box, *sems, hub)

        @pl.when(c == 1)
        def _():
            box[...] = col_share(part, c_mine)[...]

    def reduced(it, h, core):
        inbox = rs_col.at[it, h, core]
        sem = rs_recv.at[2 * it + 1, h, core]
        wait_bytes(inbox.at[pl.ds(0, n_src - core)], sem)
        return blocks_of((lb_low, lb_v)[core], c_rows, h) * LOG2E - lse2(inbox[...])

    def settle_cols(it):
        @pl.when(c == 1)
        def _():
            for h in (0, 1):
                there = col_share(pots.at[2 * it + 2, h], c_mine)
                recv = ag_recv.at[2 * it + 1, h]
                low = g_low.at[it, h]
                low[...] = reduced(it, h, 0)
                for d in col_near:
                    remote(low, there, ag_send.at[2 * it + 1, h, 0], recv, col_low(d))
                remote(low, there, ag_send.at[2 * it + 1, h, 0], recv, low_core)
                there[...] = reduced(it, h, 1)
                for d in col_near:
                    remote(there, there, ag_send.at[2 * it + 1, h, 1], recv, col_hub(d))

    def wait_cols(it, h):
        pot, sem = pots.at[2 * it + 2, h], ag_recv.at[2 * it + 1, h]

        @pl.when(c == 0)
        def _():
            wait_bytes(pot, sem)

        @pl.when(c == 1)
        def _():
            wait_bytes(pot.at[pl.ds(0, 128 - c_rows)], sem)

    def last_cols(it):
        home = g_out.at[pl.ds(pl.multiple_of(c_mine * 2 * c_rows, 2 * c_rows), 2 * c_rows)]
        recv = ag_recv.at[2 * it + 1, 0]

        @pl.when(c == 1)
        def _():
            for core in (0, 1):
                for h in (0, 1):
                    g_last[core, pl.ds(h, c_rows, stride=2), :] = reduced(it, h, core) * LN2
                send = ag_send.at[2 * it + 1, 0, core]
                for d in col_near:
                    remote(g_last.at[core], home, send, recv, (col_low, col_hub)[core](d))
                if core == 0:
                    remote(g_last.at[0], home, send, recv, low_core)
            keep = pltpu.make_async_copy(g_last.at[1], home, out_sem)
            keep.start()
            keep.wait()
            wait_bytes(g_out.at[pl.ds(0, 256 - 2 * c_rows)], recv)

        @pl.when(c == 0)
        def _():
            wait_bytes(g_out, recv)

    mrun[16 * slots : 16 * slots + 8, :] = jnp.full((8, 128), -1e30, jnp.float32)
    for it in range(ITERS):
        for q in (0, 1):
            if it > 0:
                wait_cols(it - 1, q)
            gather(pots.at[2 * it, q], back_c, q)
            if it > 0:
                sweep(kt, q, (0, 1) if q == 0 else (0,), q == 1)
        if it == 0:
            first_sweep()
        fold(0, into_r, back_r, parts.at[2 * it, 0])
        if it == 0:
            pl.semaphore_wait(barrier, jnp.where(c == 1, 2 * (n_z - 1) + 2 * (n_src - 1) + 1, n_z + n_src - 1))
        send_rows(it, 0)
        sweep_kept(kt, 1, (1,))
        fold(1, into_r, back_r, parts.at[2 * it, 1])
        send_rows(it, 1)
        if it == 0:
            la_copy.wait()
            lb_copy.wait()

            @pl.when(c == 0)
            def _():
                remote(lb_v, lb_low, lb_sem, lb_rsem, hub)

            lax.fori_loop(0, n_chunks, widen_tiles, 0)
        settle_rows(it)
        for q in (0, 1):
            wait_rows(it, q)
            gather(pots.at[2 * it + 1, q], back_r, q)
            sweep(kf, q, (0, 1) if q == 0 else (0,), q == 1)
        fold(0, into_c, back_c, parts.at[2 * it + 1, 0])
        send_cols(it, 0)
        sweep_kept(kf, 1, (1,))
        fold(1, into_c, back_c, parts.at[2 * it + 1, 1])
        send_cols(it, 1)
        if it == 0:
            @pl.when(c == 1)
            def _():
                wait_bytes(lb_low, lb_rsem)

        if it < ITERS - 1:
            settle_cols(it)
    for h in (0, 1):
        f_out[pl.ds(h, 128, stride=2), :] = pots[2 * ITERS - 1, h] * LN2
    last_cols(ITERS - 1)

    for k in range(2 * ITERS):
        for h in (0, 1):
            sem, sent = rs_send.at[k, h], ag_send.at[k, h, 0]
            rows, cols = rs_row.at[0, 0], rs_col.at[0, 0, 0]

            @pl.when(c == 0)
            def _():
                wait_bytes(rows.at[pl.ds(0, n_z)] if k % 2 == 0 else cols, sem)

            @pl.when(c == 1)
            def _():
                if k % 2 == 0:
                    wait_bytes(rows.at[pl.ds(0, n_z - 1)], sem)
                    wait_bytes(rows.at[pl.ds(0, 2 * len(row_near) + 1)], sent)
                    return
                wait_bytes(cols.at[pl.ds(0, n_src - 1)], sem)
                if k < 2 * ITERS - 1:
                    wait_bytes(cols.at[pl.ds(0, len(col_near) + 1)], sent)
                    wait_bytes(cols.at[pl.ds(0, len(col_near))], ag_send.at[k, h, 1])
                elif h == 0:
                    wait_bytes(g_out, sent)
                    wait_bytes(g_out.at[pl.ds(0, 256 - 2 * c_rows)], ag_send.at[k, h, 1])

    @pl.when(c == 0)
    def _():
        wait_bytes(lb_v, lb_sem)


def per_device(n_src, n_tgt, log_kernel, tile_rows, tile_cols, tile_count, log_a, log_b, g_start):
    slots, width = log_kernel.shape[2], log_kernel.shape[3]
    f32 = jnp.float32
    anywhere = pl.BlockSpec(memory_space=pl.ANY)
    vmem = pl.BlockSpec(memory_space=pltpu.VMEM)
    smem = pl.BlockSpec(memory_space=pltpu.SMEM)
    r_rows, c_rows = 128 // (n_tgt // 2), 128 // (n_src // 2)
    dma = pltpu.SemaphoreType.DMA
    f, g = pl.pallas_call(
        functools.partial(whole, n_src, n_tgt),
        out_shape=(pltpu.VMEM((256, 128), f32), pltpu.VMEM((256, 128), f32)),
        in_specs=[anywhere, anywhere, anywhere, smem, anywhere, anywhere, anywhere],
        out_specs=(vmem, vmem),
        scratch_shapes=[
            pltpu.VMEM((1, slots), jnp.int32),
            pltpu.VMEM((1, slots), jnp.int32),
            pltpu.VMEM((slots, width, width), jnp.bfloat16),
            pltpu.VMEM((slots, width, width), f32),
            pltpu.VMEM((slots, width, width), f32),
            pltpu.VMEM((2 * ITERS, 2, 128, 128), f32),
            pltpu.VMEM((2 * ITERS, 2, 128, 128), f32),
            pltpu.VMEM((ITERS, 2, n_tgt, r_rows, 128), f32),
            pltpu.VMEM((ITERS, 2, 2, n_src, c_rows, 128), f32),
            pltpu.VMEM((2 * r_rows, 128), f32),
            pltpu.VMEM((2 * c_rows, 128), f32),
            pltpu.VMEM((2 * c_rows, 128), f32),
            pltpu.VMEM((ITERS, 2, c_rows, 128), f32),
            pltpu.VMEM((2, 2 * c_rows, 128), f32),
            pltpu.VMEM((256, 128), f32),
            pltpu.VMEM((2, slots, 128), f32),
            pltpu.VMEM((GROUP, 128, 128), f32),
            pltpu.VMEM((GROUP, 128, 128), f32),
            pltpu.VMEM((slots, 128, 128), f32),
            pltpu.VMEM((slots, 128, 128), f32),
            pltpu.VMEM((16 * slots + 8, 128), f32),
            pltpu.VMEM((16 * slots, 128), f32),
            pltpu.VMEM((128, slots), jnp.bfloat16),
            pltpu.VMEM((slots, 128), jnp.bfloat16),
            pltpu.VMEM((128, slots), jnp.bfloat16),
            pltpu.VMEM((slots, 128), jnp.bfloat16),
            dma((slots // CHUNK,)),
            dma((5,)),
            dma,
            dma,
            dma,
            dma((2 * ITERS, 2)),
            dma((2 * ITERS, 2, 2)),
            dma((2 * ITERS, 2, 2)),
            dma((2 * ITERS, 2)),
        ],
        compiler_params=pltpu.CompilerParams(
            collective_id=0, has_side_effects=True, vmem_limit_bytes=56 * 1024 * 1024
        ),
        name="sinkhorn",
    )(
        log_kernel.reshape(slots, width, width),
        tile_rows.reshape(1, slots),
        tile_cols.reshape(1, slots),
        tile_count,
        log_a.reshape(256, 128),
        log_b.reshape(256, 128),
        g_start.reshape(256, 128),
    )
    return f.reshape(-1), g.reshape(-1)


def solution(mesh):
    n_src, n_tgt = mesh.shape["src"], mesh.shape["tgt"]
    in_specs = (
        P("src", "tgt", None, None, None),
        P("src", "tgt", None),
        P("src", "tgt", None),
        P("src", "tgt"),
        P("src"),
        P("tgt"),
        P("tgt"),
    )
    return jax.shard_map(
        functools.partial(per_device, n_src, n_tgt),
        mesh=mesh, in_specs=in_specs, out_specs=(P("src"), P("tgt")), check_vma=False,
    )
```

```python
import functools

import jax
import jax.numpy as jnp
from jax import lax
from jax.experimental import pallas as pl
from jax.experimental.pallas import tpu as pltpu
from jax.sharding import PartitionSpec as P

ITERS = 2
TINY = 1e-37
LOG2E = 1.4426950408889634
LN2 = 0.6931471805599453
MESH = pl.DeviceIdType.MESH
GROUP = 6
CHUNK = 4

SPREAD = 8.0


def lse2(values):
    top = jnp.max(values, axis=0)
    total = jnp.sum(jnp.exp2(values - top[None]), axis=0)
    return top + log2(total)


def membership(ids_ref, count, into, back):
    slots = ids_ref.shape[1]
    block = lax.broadcasted_iota(jnp.int32, (128, slots), 0)
    slot = lax.broadcasted_iota(jnp.int32, (128, slots), 1)
    hit = (ids_ref[...] == block) & (slot < count)
    hit = jnp.where(hit, 1.0, 0.0)
    into[...] = hit.astype(jnp.bfloat16)
    back[...] = hit.T.astype(jnp.bfloat16)


def dot(a, b):
    return jnp.dot(a, b, preferred_element_type=jnp.float32)


def log2(x):
    return jnp.log(x) * LOG2E


def whole(
    n_src, n_tgt,
    k_hbm, rows_hbm, cols_hbm, count_ref, la_hbm, lb_hbm, g0_hbm,
    f_out, g_out,
    rows_ref, cols_ref, kb, kt, kf, pots, parts, rs_row, rs_col, la_v, lb_v, lb_low, g_low, g_last, g_raw, gathered, wide0, wide1,
    kept0, kept, mrun, srun, into_r, back_r, into_c, back_c,
    k_sem, in_sem, out_sem, lb_sem, lb_rsem, rs_send, rs_recv, ag_send, ag_recv,
):
    s, t = lax.axis_index("src"), lax.axis_index("tgt")
    z, c = t // 2, t % 2
    slots = kb.shape[0]
    n_chunks = slots // CHUNK
    n_z = n_tgt // 2
    r_shares, c_shares = n_z, n_src // 2
    r_rows, c_rows = 128 // r_shares, 128 // c_shares
    side = 4
    y, x = s // side, s % side

    def col_share_of(y, x):
        return (y % 2) * side + (x + 2 * (y // 2)) % side

    r_mine, c_mine = z % r_shares, col_share_of(y, x)
    low_core = (s, 2 * z)
    hub = (s, 2 * z + 1)

    def k_copy(i):
        piece = pl.ds(i * CHUNK, CHUNK)
        return pltpu.make_async_copy(k_hbm.at[piece], kb.at[piece], k_sem.at[i])

    g0_copy = pltpu.make_async_copy(g0_hbm, g_raw, in_sem.at[0])
    g0_copy.start()
    for i in range(n_chunks):
        k_copy(i).start()
    id_copies = [
        pltpu.make_async_copy(rows_hbm, rows_ref, in_sem.at[3]),
        pltpu.make_async_copy(cols_hbm, cols_ref, in_sem.at[4]),
    ]
    for copy in id_copies:
        copy.start()
    la_copy = pltpu.make_async_copy(la_hbm.at[pl.ds(2 * r_mine * r_rows, 2 * r_rows)], la_v, in_sem.at[1])
    la_copy.start()
    lb_copy = pltpu.make_async_copy(lb_hbm.at[pl.ds(2 * c_mine * c_rows, 2 * c_rows)], lb_v, in_sem.at[2])
    lb_copy.start()

    def row_hub(d):
        return (s, 2 * ((z + d) % n_z) + 1)

    def row_low(d):
        return (s, 2 * ((z + d) % n_z))

    def torus(d):
        return (y + d[0]) % side, (x + d[1]) % side

    def col_hub(d):
        return (torus(d)[0] * side + torus(d)[1], 2 * z + 1)

    def col_low(d):
        return (torus(d)[0] * side + torus(d)[1], 2 * z)

    def around(d):
        return min(d, side - d)

    row_order = sorted(range(1, n_z), key=lambda d: -min(d, n_z - d))
    row_near = row_order
    col_order = [(dy, dx) for dy in range(side) for dx in range(side) if dy or dx]
    col_order.sort(key=lambda d: -around(d[0]) - around(d[1]))
    col_near = ((0, 2), (1, 1), (1, 3), (0, 1), (0, 3), (1, 0), (3, 0))

    barrier = pltpu.get_barrier_semaphore()

    def greet(peer):
        pl.semaphore_signal(barrier, inc=1, device_id=peer, device_id_type=MESH)

    @pl.when(c == 1)
    def _():
        for d in range(1, n_z):
            greet(row_hub(d))
            greet(row_low(d))
        for d in col_order:
            greet(col_hub(d))
            greet(col_low(d))
        greet(low_core)

    @pl.when(c == 0)
    def _():
        for d in range(1, n_z):
            greet(row_hub(d))
        for d in col_order:
            greet(col_hub(d))
        greet(hub)

    for copy in id_copies:
        copy.wait()
    count = count_ref[0, 0]
    membership(rows_ref, count, into_r, back_r)
    membership(cols_ref, count, into_c, back_c)

    def blocks_of(ref, rows, h):
        return ref[pl.ds(h, rows, stride=2), :]

    g0_copy.wait()
    for h in (0, 1):
        pots[0, h] = blocks_of(g_raw, 128, h) * LOG2E

    def flip(slot):
        for p in (0, 1):
            for q in (0, 1):
                piece = kb[slot, 128 * p : 128 * p + 128, 128 * q : 128 * q + 128]
                flipped = piece.T.astype(jnp.float32) * LOG2E
                kt[slot, 128 * q : 128 * q + 128, 128 * p : 128 * p + 128] = flipped

    def widen_tiles(i, carry):
        for u in range(CHUNK):
            kf[i * CHUNK + u] = kb[i * CHUNK + u].astype(jnp.float32) * LOG2E
        return carry

    def gather(pot, pick, q):
        value = pot[...]
        rows = jnp.zeros((slots, 128), jnp.float32)
        for _ in range(3):
            piece = value.astype(jnp.bfloat16)
            rows += dot(pick[...], piece)
            value -= piece.astype(jnp.float32)
        gathered[q] = rows

    def spread(q, slot, *places):
        row = jnp.broadcast_to(gathered[q, pl.ds(slot, 1), :], (128, 128)).T
        for wide, u in places:
            wide[u] = row

    def add_up(tiles, wide, u, slot, q, halves, guard):
        for h in halves:
            x = tiles[slot, 128 * q : 128 * q + 128, 128 * h : 128 * h + 128] + wide[u]
            x = x.reshape(16, 8, 128)
            here = pl.ds(pl.multiple_of(slot * 16 + 8 * h, 8), 8)
            old = mrun[guard if q == 0 else here, :]
            top = jnp.maximum(jnp.max(x, axis=0), old)
            mrun[here, :] = top
            total = jnp.sum(jnp.exp2(x - top[None]), axis=0)
            if q == 1:
                total += srun[here, :] * jnp.exp2(old - top)
            srun[here, :] = total

    def guard_of(i):
        return pl.ds(pl.multiple_of(16 * slots + 8 * jnp.maximum(i - slots, 0), 8), 8)

    rounds = slots // (2 * GROUP)

    def sweep(tiles, q):
        keep = (kept0, kept)[q]

        def ahead(wide, u, slot):
            at = jnp.minimum(slot, slots - 1)
            spread(q, at, (wide, u), (keep, at))

        def step(halves, i, carry):
            slot = i * (2 * GROUP)
            guard = guard_of(i)
            for u in range(GROUP):
                add_up(tiles, wide0, u, slot + u, q, halves, guard)
                ahead(wide1, u, slot + GROUP + u)
            for u in range(GROUP):
                add_up(tiles, wide1, u, slot + GROUP + u, q, halves, guard)
                ahead(wide0, u, slot + 2 * GROUP + u)
            return carry

        for u in range(GROUP):
            ahead(wide0, u, u)
        middle = rounds // 2 if q == 0 else 0
        if middle:
            lax.fori_loop(0, middle, functools.partial(step, (0, 1)), 0)
        lax.fori_loop(middle, rounds, functools.partial(step, (0,)), 0)

    def first_sweep():
        def ahead(slot):
            flip(slot)
            spread(0, slot, (kept0, slot))
            spread(1, slot, (kept, slot))

        def add(i, u):
            slot = i * CHUNK + u
            add_up(kt, kept0, slot, slot, 0, (0, 1), guard_of(i))
            add_up(kt, kept, slot, slot, 1, (0,), None)

        def step(i, carry):
            k_copy(i + 1).wait()
            for u in range(CHUNK):
                add(i, u)
                ahead((i + 1) * CHUNK + u)
            return carry

        k_copy(0).wait()
        for u in range(CHUNK):
            ahead(u)
        lax.fori_loop(0, n_chunks - 1, step, 0)
        for u in range(CHUNK):
            add(n_chunks - 1, u)

    def sweep_kept(tiles, rest):
        def step(late, i, carry):
            for u in range(2 * GROUP):
                slot = i * (2 * GROUP) + u
                if late:
                    add_up(tiles, kept0, slot, slot, 0, (1,), guard_of(i))
                add_up(tiles, kept, slot, slot, 1, (1,), None)
            return carry

        middle = rounds // 2 if rest else rounds
        lax.fori_loop(0, middle, functools.partial(step, False), 0)
        if rest:
            lax.fori_loop(middle, rounds, functools.partial(step, True), 0)

    def fold(h, into, back, part):
        def over_sublanes(i):
            lines = [pl.ds(128 * i + 8 * h + k, 8, stride=16) for k in range(8)]
            tops = [mrun[p, :] for p in lines]
            top = functools.reduce(jnp.maximum, tops)
            return top + log2(sum(srun[p, :] * jnp.exp2(m - top) for p, m in zip(lines, tops)))

        lse = jnp.concatenate([over_sublanes(i) for i in range(slots // 8)], axis=0)
        live = lax.broadcasted_iota(jnp.int32, (slots, 128), 0) < count
        lse = jnp.where(live, lse, -2000.0)
        gauge = dot(into[...], jnp.exp2(lse * (1.0 / SPREAD)).astype(jnp.bfloat16))
        level = (SPREAD * log2(gauge + TINY)).astype(jnp.bfloat16)
        scaled = jnp.exp2(lse - dot(back[...], level))
        coarse = scaled.astype(jnp.bfloat16)
        fine = (scaled - coarse.astype(jnp.float32)).astype(jnp.bfloat16)
        total = dot(into[...], coarse) + dot(into[...], fine)
        part[...] = level.astype(jnp.float32) + log2(total + TINY)

    def remote(src, dst, send, recv, peer):
        pltpu.make_async_remote_copy(
            src_ref=src, dst_ref=dst, send_sem=send, recv_sem=recv, device_id=peer, device_id_type=MESH
        ).start()

    def wait_bytes(ref, sem):
        pltpu.make_async_copy(ref, ref, sem).wait()

    def row_share(ref, owner):
        return ref.at[pl.ds(pl.multiple_of(owner * r_rows, r_rows), r_rows), :]

    def col_share(ref, owner):
        return ref.at[pl.ds(pl.multiple_of(owner * c_rows, c_rows), c_rows), :]

    def send_rows(it, h):
        part, box = parts.at[2 * it, h], rs_row.at[it, h, t]
        sems = rs_send.at[2 * it, h], rs_recv.at[2 * it, h, 0]
        for d in row_order:
            remote(row_share(part, (z + d) % r_shares), box, *sems, row_hub(d))

        @pl.when(c == 0)
        def _():
            remote(row_share(part, r_mine), box, *sems, hub)

        @pl.when(c == 1)
        def _():
            box[...] = row_share(part, r_mine)[...]

    def settle_rows(it):
        @pl.when(c == 1)
        def _():
            for h in (0, 1):
                inbox = rs_row.at[it, h]
                mine = row_share(pots.at[2 * it + 1, h], r_mine)
                sems = ag_send.at[2 * it, h, 0], ag_recv.at[2 * it, h]
                wait_bytes(inbox.at[pl.ds(0, n_tgt - 1)], rs_recv.at[2 * it, h, 0])
                mine[...] = blocks_of(la_v, r_rows, h) * LOG2E - lse2(inbox[...])
                for d in row_near:
                    remote(mine, mine, *sems, row_low(d))
                    remote(mine, mine, *sems, row_hub(d))
                remote(mine, mine, *sems, low_core)

    def wait_rows(it, h):
        pot, sem = pots.at[2 * it + 1, h], ag_recv.at[2 * it, h]

        @pl.when(c == 0)
        def _():
            wait_bytes(pot, sem)

        @pl.when(c == 1)
        def _():
            wait_bytes(pot.at[pl.ds(0, 128 - r_rows)], sem)

    def send_cols(it, h):
        part, box = parts.at[2 * it + 1, h], rs_col.at[it, h, c, s]
        sems = rs_send.at[2 * it + 1, h], rs_recv.at[2 * it + 1, h, c]
        for d in col_order:
            remote(col_share(part, col_share_of(*torus(d))), box, *sems, col_hub(d))

        @pl.when(c == 0)
        def _():
            remote(col_share(part, c_mine), box, *sems, hub)

        @pl.when(c == 1)
        def _():
            box[...] = col_share(part, c_mine)[...]

    def reduced(it, h, core):
        inbox = rs_col.at[it, h, core]
        sem = rs_recv.at[2 * it + 1, h, core]
        wait_bytes(inbox.at[pl.ds(0, n_src - core)], sem)
        return blocks_of((lb_low, lb_v)[core], c_rows, h) * LOG2E - lse2(inbox[...])

    def settle_cols(it):
        @pl.when(c == 1)
        def _():
            for h in (0, 1):
                there = col_share(pots.at[2 * it + 2, h], c_mine)
                recv = ag_recv.at[2 * it + 1, h]
                low = g_low.at[it, h]
                low[...] = reduced(it, h, 0)
                for d in col_near:
                    remote(low, there, ag_send.at[2 * it + 1, h, 0], recv, col_low(d))
                remote(low, there, ag_send.at[2 * it + 1, h, 0], recv, low_core)
                there[...] = reduced(it, h, 1)
                for d in col_near:
                    remote(there, there, ag_send.at[2 * it + 1, h, 1], recv, col_hub(d))

    def wait_cols(it, h):
        pot, sem = pots.at[2 * it + 2, h], ag_recv.at[2 * it + 1, h]

        @pl.when(c == 0)
        def _():
            wait_bytes(pot, sem)

        @pl.when(c == 1)
        def _():
            wait_bytes(pot.at[pl.ds(0, 128 - c_rows)], sem)

    def last_cols(it):
        home = g_out.at[pl.ds(pl.multiple_of(c_mine * 2 * c_rows, 2 * c_rows), 2 * c_rows)]
        recv = ag_recv.at[2 * it + 1, 0]

        @pl.when(c == 1)
        def _():
            for core in (0, 1):
                for h in (0, 1):
                    g_last[core, pl.ds(h, c_rows, stride=2), :] = reduced(it, h, core) * LN2
                send = ag_send.at[2 * it + 1, 0, core]
                for d in col_near:
                    remote(g_last.at[core], home, send, recv, (col_low, col_hub)[core](d))
                if core == 0:
                    remote(g_last.at[0], home, send, recv, low_core)
            keep = pltpu.make_async_copy(g_last.at[1], home, out_sem)
            keep.start()
            keep.wait()
            wait_bytes(g_out.at[pl.ds(0, 256 - 2 * c_rows)], recv)

        @pl.when(c == 0)
        def _():
            wait_bytes(g_out, recv)

    mrun[16 * slots : 16 * slots + 8, :] = jnp.full((8, 128), -1e30, jnp.float32)
    for it in range(ITERS):
        for q in (0, 1):
            if it > 0:
                wait_cols(it - 1, q)
            gather(pots.at[2 * it, q], back_c, q)
            if it > 0:
                sweep(kt, q)
        if it == 0:
            first_sweep()
        fold(0, into_r, back_r, parts.at[2 * it, 0])
        if it == 0:
            pl.semaphore_wait(barrier, jnp.where(c == 1, 2 * (n_z - 1) + 2 * (n_src - 1) + 1, n_z + n_src - 1))
        send_rows(it, 0)
        sweep_kept(kt, it > 0)
        fold(1, into_r, back_r, parts.at[2 * it, 1])
        send_rows(it, 1)
        if it == 0:
            la_copy.wait()
            lb_copy.wait()

            @pl.when(c == 0)
            def _():
                remote(lb_v, lb_low, lb_sem, lb_rsem, hub)

            lax.fori_loop(0, n_chunks, widen_tiles, 0)
        settle_rows(it)
        for q in (0, 1):
            wait_rows(it, q)
            gather(pots.at[2 * it + 1, q], back_r, q)
            sweep(kf, q)
        fold(0, into_c, back_c, parts.at[2 * it + 1, 0])
        send_cols(it, 0)
        sweep_kept(kf, True)
        fold(1, into_c, back_c, parts.at[2 * it + 1, 1])
        send_cols(it, 1)
        if it == 0:
            @pl.when(c == 1)
            def _():
                wait_bytes(lb_low, lb_rsem)

        if it < ITERS - 1:
            settle_cols(it)
    for h in (0, 1):
        f_out[pl.ds(h, 128, stride=2), :] = pots[2 * ITERS - 1, h] * LN2
    last_cols(ITERS - 1)

    for k in range(2 * ITERS):
        for h in (0, 1):
            sem, sent = rs_send.at[k, h], ag_send.at[k, h, 0]
            rows, cols = rs_row.at[0, 0], rs_col.at[0, 0, 0]

            @pl.when(c == 0)
            def _():
                wait_bytes(rows.at[pl.ds(0, n_z)] if k % 2 == 0 else cols, sem)

            @pl.when(c == 1)
            def _():
                if k % 2 == 0:
                    wait_bytes(rows.at[pl.ds(0, n_z - 1)], sem)
                    wait_bytes(rows.at[pl.ds(0, 2 * len(row_near) + 1)], sent)
                    return
                wait_bytes(cols.at[pl.ds(0, n_src - 1)], sem)
                if k < 2 * ITERS - 1:
                    wait_bytes(cols.at[pl.ds(0, len(col_near) + 1)], sent)
                    wait_bytes(cols.at[pl.ds(0, len(col_near))], ag_send.at[k, h, 1])
                elif h == 0:
                    wait_bytes(g_out, sent)
                    wait_bytes(g_out.at[pl.ds(0, 256 - 2 * c_rows)], ag_send.at[k, h, 1])

    @pl.when(c == 0)
    def _():
        wait_bytes(lb_v, lb_sem)


def per_device(n_src, n_tgt, log_kernel, tile_rows, tile_cols, tile_count, log_a, log_b, g_start):
    slots, width = log_kernel.shape[2], log_kernel.shape[3]
    f32 = jnp.float32
    anywhere = pl.BlockSpec(memory_space=pl.ANY)
    vmem = pl.BlockSpec(memory_space=pltpu.VMEM)
    smem = pl.BlockSpec(memory_space=pltpu.SMEM)
    r_rows, c_rows = 128 // (n_tgt // 2), 128 // (n_src // 2)
    dma = pltpu.SemaphoreType.DMA
    f, g = pl.pallas_call(
        functools.partial(whole, n_src, n_tgt),
        out_shape=(pltpu.VMEM((256, 128), f32), pltpu.VMEM((256, 128), f32)),
        in_specs=[anywhere, anywhere, anywhere, smem, anywhere, anywhere, anywhere],
        out_specs=(vmem, vmem),
        scratch_shapes=[
            pltpu.VMEM((1, slots), jnp.int32),
            pltpu.VMEM((1, slots), jnp.int32),
            pltpu.VMEM((slots, width, width), jnp.bfloat16),
            pltpu.VMEM((slots, width, width), f32),
            pltpu.VMEM((slots, width, width), f32),
            pltpu.VMEM((2 * ITERS, 2, 128, 128), f32),
            pltpu.VMEM((2 * ITERS, 2, 128, 128), f32),
            pltpu.VMEM((ITERS, 2, n_tgt, r_rows, 128), f32),
            pltpu.VMEM((ITERS, 2, 2, n_src, c_rows, 128), f32),
            pltpu.VMEM((2 * r_rows, 128), f32),
            pltpu.VMEM((2 * c_rows, 128), f32),
            pltpu.VMEM((2 * c_rows, 128), f32),
            pltpu.VMEM((ITERS, 2, c_rows, 128), f32),
            pltpu.VMEM((2, 2 * c_rows, 128), f32),
            pltpu.VMEM((256, 128), f32),
            pltpu.VMEM((2, slots, 128), f32),
            pltpu.VMEM((GROUP, 128, 128), f32),
            pltpu.VMEM((GROUP, 128, 128), f32),
            pltpu.VMEM((slots, 128, 128), f32),
            pltpu.VMEM((slots, 128, 128), f32),
            pltpu.VMEM((16 * slots + 8, 128), f32),
            pltpu.VMEM((16 * slots, 128), f32),
            pltpu.VMEM((128, slots), jnp.bfloat16),
            pltpu.VMEM((slots, 128), jnp.bfloat16),
            pltpu.VMEM((128, slots), jnp.bfloat16),
            pltpu.VMEM((slots, 128), jnp.bfloat16),
            dma((slots // CHUNK,)),
            dma((5,)),
            dma,
            dma,
            dma,
            dma((2 * ITERS, 2)),
            dma((2 * ITERS, 2, 2)),
            dma((2 * ITERS, 2, 2)),
            dma((2 * ITERS, 2)),
        ],
        compiler_params=pltpu.CompilerParams(
            collective_id=0, has_side_effects=True, vmem_limit_bytes=56 * 1024 * 1024
        ),
        name="sinkhorn",
    )(
        log_kernel.reshape(slots, width, width),
        tile_rows.reshape(1, slots),
        tile_cols.reshape(1, slots),
        tile_count,
        log_a.reshape(256, 128),
        log_b.reshape(256, 128),
        g_start.reshape(256, 128),
    )
    return f.reshape(-1), g.reshape(-1)


def solution(mesh):
    n_src, n_tgt = mesh.shape["src"], mesh.shape["tgt"]
    in_specs = (
        P("src", "tgt", None, None, None),
        P("src", "tgt", None),
        P("src", "tgt", None),
        P("src", "tgt"),
        P("src"),
        P("tgt"),
        P("tgt"),
    )
    return jax.shard_map(
        functools.partial(per_device, n_src, n_tgt),
        mesh=mesh, in_specs=in_specs, out_specs=(P("src"), P("tgt")), check_vma=False,
    )
```
